32 devices in a mesh: groups: 2 (over y), tok: 4 (over x, core), hid: 4 (over z).
Axes of the slice: x: 2, y: 2, z: 4, core: 2. Of those that a mesh axis runs over, the one named last changes fastest.
Arguments:
- states: bfloat16 [8192, 5376], P(('groups', 'tok'), 'hid'), parts along dimension 0, may hold values from -6 to 6
- w_qkv: bfloat16 [5376, 8, 512], P('tok', 'hid'), may hold values from -0.078125 to 0.078125
- w_out: bfloat16 [2048, 5376], P('tok', 'hid'), may hold values from -0.125 to 0.125
- q_gain: float32 [128], replicated, may hold values from 0.5 to 14, as said below
- k_gain: float32 [128], replicated, may hold values from 0.5 to 14, as said below
Outputs:
- attended: bfloat16 [8192, 5376], P(('groups', 'tok'), 'hid'), parts along dimension 0
The draws below stay inside these ranges and needn't reach their ends.
There are 2 independent parts, one for each index of `groups`. The reference program is written for one: setup_inputs(seed, part) draws one part's arguments, and reference() takes and returns one part's arrays. A program takes and returns all parts, laid end to end along the dimension named above; an argument that names none is the same for every part. Nothing has to cross between parts.
Inputs may be any that keep to these rules, and one draw needn't show every extreme that they name: `q_gain`: entries are positive. `k_gain`: entries are positive.
All inputs are finite; a program needn't handle non-finite values.
Results may differ from the reference program's by a relative error of at most 0.017.
The reference program's roundings to bfloat16 on the way count: a program that leaves them out, or rounds other values in their place, can miss the bound.
Values may be sent and summed in bfloat16 or wider, within the bound.
A program may use at most 128 MiB of HBM per device.

```python
import math
import jax
import jax.numpy as jnp
from jax import lax

D = 5376
HD = 128
KV_HEADS = 8
GROUP = 2
WINDOW = 1024
SEQ = 4096


def gain_draw(key):
    uniform_part = jax.random.uniform(key, (HD,), jnp.float32)
    return jnp.exp(jnp.log(0.5) + uniform_part * jnp.log(4.0))


def draw_q_gain(key, part):
    return gain_draw(jax.random.fold_in(key, 11))


def draw_k_gain(key, part):
    return gain_draw(jax.random.fold_in(key, 23))


def shard_levels(rng, extent, split, least, top_value):
    loudness = 1.0
    for axis_at, blocks in split:
        draws = jax.random.uniform(jax.random.fold_in(jax.random.fold_in(rng, 6), axis_at), (blocks,), jnp.float32, least / len(split), top_value / len(split))
        loudness = loudness * jnp.repeat(jnp.exp(draws), extent[axis_at] // blocks).reshape((-1,) + (1,) * (len(extent) - 1 - axis_at))
    return loudness


def bell_draw(key, extent, deviation, reach, shards=(), held_as=jnp.bfloat16):
    factor_of = shard_levels(key, extent, shards, -0.22, 0.18) if shards else 1.0
    drawn = jax.random.normal(key, extent, jnp.float32) * deviation * factor_of
    return jnp.minimum(jnp.maximum(drawn, -reach), reach).astype(held_as)


def setup_inputs(seed: int = 0, part: int = 0) -> dict:
    key_of = jax.random.split(jax.random.key(seed), 6)
    own_keys = jax.random.split(jax.random.fold_in(key_of[5], part), 6)
    return {
        "states": bell_draw(own_keys[0], (SEQ, D), 1.0, 6.0, ((0, 4), (1, 4))),
        "w_qkv": bell_draw(key_of[1], (D, KV_HEADS, (GROUP + 2) * HD), D ** -0.5, 0.078125, ((0, 4), (1, 4))),
        "w_out": bell_draw(key_of[2], (KV_HEADS * GROUP * HD, D), (KV_HEADS * GROUP * HD) ** -0.5, 0.125, ((0, 4), (1, 4))),
        "q_gain": draw_q_gain(jax.random.fold_in(key_of[5], 71), part),
        "k_gain": draw_k_gain(jax.random.fold_in(key_of[5], 71), part),
    }


EPS = 1e-06
SCALE = 168.0 ** (-0.5)
ROPE_BASE = 10000.0

def head_norm(values, gain):
    meansq = lax.optimization_barrier(jnp.mean(values * values, axis=-1, keepdims=True))
    return values * lax.rsqrt(meansq + EPS) * gain

def rotate(values, pos):
    half = values.shape[-1] // 2
    inverse = jnp.exp(jnp.arange(half, dtype=jnp.float32) * (-2.0 * math.log(ROPE_BASE) / values.shape[-1]))
    angle = pos.astype(jnp.float32)[:, None] * inverse[None, :]
    shape = (angle.shape[0],) + (1,) * (values.ndim - 2) + (half,)
    cosine = jnp.cos(angle).reshape(shape)
    sine = jnp.sin(angle).reshape(shape)
    first = values[..., :half]
    second = values[..., half:]
    return jnp.concatenate([first * cosine - second * sine, second * cosine + first * sine], axis=-1)

def project(states, w_qkv, q_gain, k_gain, pos):
    rows = states.shape[0]
    kv_local = w_qkv.shape[1]
    qkv = jnp.dot(states, w_qkv.reshape(w_qkv.shape[0], -1), preferred_element_type=jnp.float32)
    qkv = qkv.reshape(rows, kv_local, GROUP + 2, HD)
    query = rotate(head_norm(qkv[:, :, :GROUP], q_gain), pos).astype(jnp.bfloat16)
    keys = rotate(head_norm(qkv[:, :, GROUP], k_gain), pos).astype(jnp.bfloat16)
    values = qkv[:, :, GROUP + 1].astype(jnp.bfloat16)
    return (query, keys, values)

def attend(query, keys, values, q_first, k_first):
    scores = jnp.einsum('qhgd,khd->hgqk', query.astype(jnp.float32), keys.astype(jnp.float32)) * SCALE
    q_index = q_first + jnp.arange(query.shape[0], dtype=jnp.int32)
    k_index = k_first + jnp.arange(keys.shape[0], dtype=jnp.int32)
    keep = (k_index[None, :] <= q_index[:, None]) & (q_index[:, None] - k_index[None, :] < WINDOW) & (k_index[None, :] >= 0)
    masked = jnp.where(keep, scores, jnp.float32(-1e+30))
    top = lax.optimization_barrier(jnp.max(masked, axis=-1, keepdims=True))
    expo = jnp.where(keep, jnp.exp(masked - top), jnp.float32(0.0))
    total = lax.optimization_barrier(jnp.sum(expo, axis=-1, keepdims=True))
    weights = (expo / total).astype(jnp.bfloat16)
    result = jnp.einsum('hgqk,khd->qhgd', weights.astype(jnp.float32), values.astype(jnp.float32))
    return result.astype(jnp.bfloat16)

def reference(states, w_qkv, w_out, q_gain, k_gain):
    pos = jnp.arange(SEQ, dtype=jnp.int32)
    query, keys, values = project(states, w_qkv, q_gain, k_gain, pos)
    block = WINDOW
    padding = jnp.zeros((block,) + keys.shape[1:], jnp.bfloat16)
    keys_pad = jnp.concatenate([padding, keys], axis=0)
    values_pad = jnp.concatenate([padding, values], axis=0)

    def one_block(index):
        start = (index * block).astype(jnp.int32)
        q_block = lax.dynamic_slice_in_dim(query, start, block, 0)
        k_block = lax.dynamic_slice_in_dim(keys_pad, start, 2 * block, 0)
        v_block = lax.dynamic_slice_in_dim(values_pad, start, 2 * block, 0)
        return attend(q_block, k_block, v_block, start, start - block)
    blocks = lax.map(one_block, jnp.arange(SEQ // block, dtype=jnp.int32))
    heads_out = blocks.reshape(SEQ, -1)
    return jnp.dot(heads_out, w_out, preferred_element_type=jnp.float32).astype(jnp.bfloat16)
```

```python
import math

import jax
import jax.numpy as jnp
from jax import lax
from jax.sharding import PartitionSpec as P

HD = 128
GROUP = 2
WINDOW = 1024


EPS = 1e-06
SCALE = 168.0 ** (-0.5)
ROPE_BASE = 10000.0


def from_behind(value, axis, steps):
    count = lax.axis_size(axis)
    first, last = (max(0, -steps), min(count, count - steps))
    return lax.ppermute(value, axis, [(source, source + steps) for source in range(first, last)])


def head_norm(values, gain):
    meansq = jnp.mean(values * values, axis=-1, keepdims=True)
    return values * lax.rsqrt(meansq + EPS) * gain


def rotate(values, pos):
    half = values.shape[-1] // 2
    inverse = jnp.exp(
        jnp.arange(half, dtype=jnp.float32) * (-2.0 * math.log(ROPE_BASE) / values.shape[-1])
    )
    angle = pos.astype(jnp.float32)[:, None] * inverse[None, :]
    shape = (angle.shape[0],) + (1,) * (values.ndim - 2) + (half,)
    cosine = jnp.cos(angle).reshape(shape)
    sine = jnp.sin(angle).reshape(shape)
    first = values[..., :half]
    second = values[..., half:]
    return jnp.concatenate(
        [first * cosine - second * sine, second * cosine + first * sine], axis=-1
    )


def attend(query, keys, values, q_first, k_first):
    scores = jnp.einsum("qhgd,khd->hgqk", query, keys, preferred_element_type=jnp.float32) * SCALE
    q_index = q_first + jnp.arange(query.shape[0], dtype=jnp.int32)
    k_index = k_first + jnp.arange(keys.shape[0], dtype=jnp.int32)
    keep = (
        (k_index[None, :] <= q_index[:, None])
        & (q_index[:, None] - k_index[None, :] < WINDOW)
        & (k_index[None, :] >= 0)
    )
    masked = jnp.where(keep, scores, jnp.float32(-1e30))
    top = jnp.max(masked, axis=-1, keepdims=True)
    expo = jnp.where(keep, jnp.exp(masked - top), jnp.float32(0.0))
    total = jnp.sum(expo, axis=-1, keepdims=True)
    weights = (expo / total).astype(jnp.bfloat16)
    result = jnp.einsum("hgqk,khd->qhgd", weights, values, preferred_element_type=jnp.float32)
    return result.astype(jnp.bfloat16)


def line_gather_dot(blocks, weight, axis):
    count = lax.axis_size(axis)
    here = lax.axis_index(axis)
    depth = blocks[0].shape[1]

    def term(block, owner):
        rows = lax.dynamic_slice_in_dim(weight, owner * depth, depth, 0)
        return jnp.dot(block, rows, preferred_element_type=jnp.float32)

    results = []
    for block in blocks:
        up = down = block
        total = term(block, here)
        for step in range(1, count):
            up = lax.ppermute(up, axis, [(i, i + 1) for i in range(step - 1, count - 1)])
            down = lax.ppermute(down, axis, [(i + 1, i) for i in range(count - step)])
            below = jnp.maximum(here - step, 0)
            above = jnp.minimum(here + step, count - 1)
            if 2 * step < count:
                total = total + term(up, below) + term(down, above)
            else:
                from_below = here >= step
                total = total + term(
                    jnp.where(from_below, up, down), jnp.where(from_below, below, above)
                )
        results.append(total)
    return results


def on_device(states, w_qkv, w_out, q_gain, k_gain):
    rows = states.shape[0]
    kv_local = w_qkv.shape[1]
    columns = kv_local * (GROUP + 2) * HD
    weight_whole = lax.all_gather(w_qkv.reshape(-1, columns), "tok", axis=0, tiled=True)
    (qkv,) = line_gather_dot([states], weight_whole, "hid")
    qkv = qkv.reshape(rows, kv_local, GROUP + 2, HD)
    base = lax.axis_index("tok") * rows
    pos = base + jnp.arange(rows, dtype=jnp.int32)
    query = rotate(head_norm(qkv[:, :, :GROUP], q_gain), pos).astype(jnp.bfloat16)
    keys = rotate(head_norm(qkv[:, :, GROUP], k_gain), pos).astype(jnp.bfloat16)
    values = qkv[:, :, GROUP + 1].astype(jnp.bfloat16)
    paired = jnp.stack([keys, values], axis=1).reshape(rows, 2 * kv_local * HD)
    hops = max(1, WINDOW // rows)
    reach = min(WINDOW, rows)
    pieces = []
    current = paired
    current = from_behind(current, "tok", 1)
    pieces.insert(0, current)
    combined = jnp.concatenate(pieces + [paired], axis=0).reshape(-1, 2, kv_local, HD)
    reach_back = hops * reach
    block = 512
    outputs = []
    for index in range(rows // block):
        q_block = query[index * block : (index + 1) * block]
        kv_block = combined[index * block : index * block + block + reach_back]
        outputs.append(
            attend(
                q_block,
                kv_block[:, 0],
                kv_block[:, 1],
                base + index * block,
                base + index * block - reach_back,
            ).reshape(block, kv_local * GROUP * HD)
        )
    out_whole = lax.all_gather(w_out, "tok", axis=0, tiled=True)
    summed = line_gather_dot(outputs, out_whole, "hid")
    return jnp.concatenate([part.astype(jnp.bfloat16) for part in summed], axis=0)


def solution(mesh):
    return jax.shard_map(
        on_device,
        mesh=mesh,
        in_specs=(P(("groups", "tok"), "hid"), P("tok", "hid", None), P("tok", "hid"), P(), P()),
        out_specs=P(("groups", "tok"), "hid"),
        check_vma=False,
    )
```

```python
import functools
import math

import jax
import jax.numpy as jnp
from jax import lax
from jax.experimental import pallas as pl
from jax.experimental.pallas import tpu as pltpu
from jax.sharding import PartitionSpec as P

HD = 128
GROUP = 2
WINDOW = 1024


EPS = 1e-06
SCALE = 168.0 ** (-0.5)
ROPE_BASE = 10000.0
PIECES = 2
CHUNKS = 2


def from_behind(value, axis, steps):
    count = lax.axis_size(axis)
    first, last = (max(0, -steps), min(count, count - steps))
    return lax.ppermute(value, axis, [(source, source + steps) for source in range(first, last)])


def rope_tables(rows, base):
    half = HD // 2
    inverse = jnp.exp(
        jnp.arange(half, dtype=jnp.float32) * (-2.0 * math.log(ROPE_BASE) / HD)
    )
    pos = base + jnp.arange(rows, dtype=jnp.int32)
    angle = pos.astype(jnp.float32)[:, None] * inverse[None, :]
    cosine, sine = jnp.cos(angle), jnp.sin(angle)
    return (
        jnp.concatenate([cosine, cosine], axis=1),
        jnp.concatenate([-sine, sine], axis=1),
    )


def norm_rope_kernel(rotated, total, x_ref, gain_ref, cos_ref, sin_ref, o_ref):
    gain = gain_ref[...]
    cosine, sine = cos_ref[...], sin_ref[...]
    for head in range(x_ref.shape[1] // HD):
        columns = slice(head * HD, (head + 1) * HD)
        values = x_ref[:, columns]
        if head % total < rotated:
            meansq = jnp.mean(values * values, axis=-1, keepdims=True)
            values = values * lax.rsqrt(meansq + EPS) * gain
            values = values * cosine + pltpu.roll(values, HD // 2, 1) * sine
        o_ref[:, columns] = values.astype(o_ref.dtype)


def norm_rope(values, gain, cosine, sine, rotated, total):
    rows, columns = values.shape
    tile = 256
    row = lambda i: (i, 0)
    return pl.pallas_call(
        functools.partial(norm_rope_kernel, rotated, total),
        out_shape=jax.ShapeDtypeStruct((rows, columns), jnp.bfloat16),
        grid=(rows // tile,),
        in_specs=[
            pl.BlockSpec((tile, columns), row),
            pl.BlockSpec((1, HD), lambda i: (0, 0)),
            pl.BlockSpec((tile, HD), row),
            pl.BlockSpec((tile, HD), row),
        ],
        out_specs=pl.BlockSpec((tile, columns), row),
        cost_estimate=pl.CostEstimate(
            flops=20 * rows * columns, bytes_accessed=6 * rows * columns, transcendentals=0
        ),
    )(values, gain.reshape(1, HD), cosine, sine)


def attend_kernel(q_tile, row0, base_ref, q_ref, k_ref, v_ref, o_ref):
    first = row0 + pl.program_id(1) * q_tile
    span = q_tile + WINDOW
    keys = k_ref[pl.ds(pl.multiple_of(first, q_tile), span), :]
    values = v_ref[pl.ds(pl.multiple_of(first, q_tile), span), :]
    row = lax.broadcasted_iota(jnp.int32, (q_tile, span), 0)
    column = lax.broadcasted_iota(jnp.int32, (q_tile, span), 1)
    least = jnp.maximum(row, WINDOW - 1 - (base_ref[0] + first))
    keep = (column > least) & (column <= row + WINDOW)
    for member in range(GROUP):
        columns = slice(member * HD, (member + 1) * HD)
        scores = lax.dot_general(
            q_ref[:, columns], keys, (((1,), (1,)), ((), ())), preferred_element_type=jnp.float32
        )
        masked = jnp.where(keep, scores, jnp.float32(-1e30))
        top = jnp.max(masked, axis=-1, keepdims=True)
        expo = jnp.exp2((masked - top) * jnp.float32(SCALE * math.log2(math.e)))
        total = jnp.sum(expo, axis=-1, keepdims=True)
        weights = (expo * (1.0 / total)).astype(jnp.bfloat16)
        result = jnp.dot(weights, values, preferred_element_type=jnp.float32)
        o_ref[:, columns] = result.astype(o_ref.dtype)


def attend(query, paired, base, row0, count):
    kv_local = query.shape[1] // (GROUP * HD)
    q_tile = 256
    from_tile = row0 // q_tile
    whole = paired.shape[0]
    return pl.pallas_call(
        functools.partial(attend_kernel, q_tile, row0),
        out_shape=jax.ShapeDtypeStruct((count, query.shape[1]), jnp.bfloat16),
        grid=(kv_local, count // q_tile),
        in_specs=[
            pl.BlockSpec(memory_space=pltpu.SMEM),
            pl.BlockSpec((q_tile, GROUP * HD), lambda h, i: (from_tile + i, h)),
            pl.BlockSpec((whole, HD), lambda h, i: (0, 2 * h)),
            pl.BlockSpec((whole, HD), lambda h, i: (0, 2 * h + 1)),
        ],
        out_specs=pl.BlockSpec((q_tile, GROUP * HD), lambda h, i: (i, h)),
        compiler_params=pltpu.CompilerParams(vmem_limit_bytes=32 * 1024 * 1024),
        cost_estimate=pl.CostEstimate(
            flops=4 * count * query.shape[1] * (WINDOW + q_tile),
            bytes_accessed=4 * (whole + count) * query.shape[1],
            transcendentals=count * query.shape[1] // HD * (WINDOW + q_tile),
        ),
    )(base.reshape(1), query, paired, paired)


def line_gather_dot(pieces, weight, axis, depth, column_ranges):
    count = lax.axis_size(axis)
    here = lax.axis_index(axis)

    def terms(totals, piece, owner, first):
        out = []
        for total, (start, width) in zip(totals, column_ranges):
            rows = lax.dynamic_slice(
                weight, (owner * depth + first, start), (piece.shape[1], width)
            )
            term = jnp.dot(piece, rows, preferred_element_type=jnp.float32)
            out.append(term if total is None else total + term)
        return out

    totals = [None] * len(column_ranges)
    ups = [piece for piece, _ in pieces]
    downs = list(ups)
    for piece, first in pieces:
        totals = terms(totals, piece, here, first)
    for step in range(1, count):
        for at, (_, first) in enumerate(pieces):
            up = lax.ppermute(ups[at], axis, [(i, i + 1) for i in range(step - 1, count - 1)])
            down = lax.ppermute(downs[at], axis, [(i + 1, i) for i in range(count - step)])
            ups[at], downs[at] = up, down
            if step == count - 1 and len(totals) > 1:
                totals, up, down = lax.optimization_barrier((totals, up, down))
            below = jnp.maximum(here - step, 0)
            above = jnp.minimum(here + step, count - 1)
            if 2 * step < count:
                totals = terms(totals, up, below, first)
                totals = terms(totals, down, above, first)
            else:
                from_below = here >= step
                totals = terms(
                    totals,
                    jnp.where(from_below, up, down),
                    jnp.where(from_below, below, above),
                    first,
                )
    return totals


def on_device(states, w_qkv, w_out, q_gain, k_gain):
    rows, depth = states.shape
    kv_local = w_qkv.shape[1]
    q_columns = kv_local * GROUP * HD
    kv_columns = kv_local * 2 * HD
    arranged = jnp.concatenate(
        [
            w_qkv[:, :, : GROUP * HD].reshape(-1, q_columns),
            w_qkv[:, :, GROUP * HD :].reshape(-1, kv_columns),
        ],
        axis=1,
    )
    weight_whole = lax.all_gather(arranged, "tok", axis=0, tiled=True)
    part = depth // PIECES
    kv, query = line_gather_dot(
        [(states[:, i * part : (i + 1) * part], i * part) for i in range(PIECES)],
        weight_whole,
        "hid",
        depth,
        [(q_columns, kv_columns), (0, q_columns)],
    )
    base = lax.axis_index("tok") * rows
    cosine, sine = rope_tables(rows, base)
    paired = norm_rope(kv, k_gain, cosine, sine, 1, 2)
    behind = from_behind(paired[rows - WINDOW :], "tok", 1)
    query = norm_rope(query, q_gain, cosine, sine, 1, 1)
    combined = jnp.concatenate([behind, paired], axis=0)
    block = rows // CHUNKS
    out_whole = lax.all_gather(w_out, "tok", axis=0, tiled=True)
    results = []
    for index in range(CHUNKS):
        heads = attend(query, combined, base, index * block, block)
        (summed,) = line_gather_dot(
            [(heads, 0)], out_whole, "hid", heads.shape[1], [(0, w_out.shape[1])]
        )
        results.append(summed.astype(jnp.bfloat16))
    return jnp.concatenate(results, axis=0)


def solution(mesh):
    return jax.shard_map(
        on_device,
        mesh=mesh,
        in_specs=(P(("groups", "tok"), "hid"), P("tok", "hid", None), P("tok", "hid"), P(), P()),
        out_specs=P(("groups", "tok"), "hid"),
        check_vma=False,
    )
```

```python
import functools
import math

import jax
import jax.numpy as jnp
from jax import lax
from jax.experimental import pallas as pl
from jax.experimental.pallas import tpu as pltpu
from jax.sharding import PartitionSpec as P

HD = 128
GROUP = 2
WINDOW = 1024


EPS = 1e-06
SCALE = 168.0 ** (-0.5)
ROPE_BASE = 10000.0
PIECES = 2


def from_behind(value, axis, steps):
    count = lax.axis_size(axis)
    first, last = (max(0, -steps), min(count, count - steps))
    return lax.ppermute(value, axis, [(source, source + steps) for source in range(first, last)])


def rope_tables(rows, base):
    half = HD // 2
    inverse = jnp.exp(
        jnp.arange(half, dtype=jnp.float32) * (-2.0 * math.log(ROPE_BASE) / HD)
    )
    pos = base + jnp.arange(rows, dtype=jnp.int32)
    angle = pos.astype(jnp.float32)[:, None] * inverse[None, :]
    cosine, sine = jnp.cos(angle), jnp.sin(angle)
    return (
        jnp.concatenate([cosine, cosine], axis=1),
        jnp.concatenate([-sine, sine], axis=1),
    )


def norm_rope_kernel(rotated, total, x_ref, gain_ref, cos_ref, sin_ref, o_ref):
    gain = gain_ref[...]
    cosine, sine = cos_ref[...], sin_ref[...]
    for head in range(x_ref.shape[1] // HD):
        columns = slice(head * HD, (head + 1) * HD)
        values = x_ref[:, columns]
        if head % total < rotated:
            meansq = jnp.mean(values * values, axis=-1, keepdims=True)
            values = values * lax.rsqrt(meansq + EPS) * gain
            values = values * cosine + pltpu.roll(values, HD // 2, 1) * sine
        o_ref[:, columns] = values.astype(o_ref.dtype)


def norm_rope(values, gain, cosine, sine, rotated, total):
    rows, columns = values.shape
    tile = 256
    row = lambda i: (i, 0)
    return pl.pallas_call(
        functools.partial(norm_rope_kernel, rotated, total),
        out_shape=jax.ShapeDtypeStruct((rows, columns), jnp.bfloat16),
        grid=(rows // tile,),
        in_specs=[
            pl.BlockSpec((tile, columns), row),
            pl.BlockSpec((1, HD), lambda i: (0, 0)),
            pl.BlockSpec((tile, HD), row),
            pl.BlockSpec((tile, HD), row),
        ],
        out_specs=pl.BlockSpec((tile, columns), row),
        cost_estimate=pl.CostEstimate(
            flops=20 * rows * columns, bytes_accessed=6 * rows * columns, transcendentals=0
        ),
    )(values, gain.reshape(1, HD), cosine, sine)


def attend_kernel(q_tile, row0, base_ref, q_ref, gain_ref, cos_ref, sin_ref, k_ref, v_ref, o_ref):
    first = row0 + pl.program_id(1) * q_tile
    parts = ((0, q_tile), (q_tile, WINDOW - q_tile), (WINDOW, q_tile))
    slices = [pl.ds(pl.multiple_of(first + start, q_tile), width) for start, width in parts]
    row = lax.broadcasted_iota(jnp.int32, (q_tile, q_tile), 0)
    column = lax.broadcasted_iota(jnp.int32, (q_tile, q_tile), 1)
    before = WINDOW - 1 - (base_ref[0] + first)
    low_keep = column > jnp.maximum(row, before)
    high_keep = column <= row
    middle = lax.broadcasted_iota(jnp.int32, (1, parts[1][1]), 1) + q_tile
    middle_bias = jnp.where(middle > before, jnp.float32(0.0), jnp.float32(-1e30))
    gain, cosine, sine = gain_ref[...], cos_ref[...], sin_ref[...]
    for member in range(GROUP):
        columns = slice(member * HD, (member + 1) * HD)
        vectors = q_ref[:, columns]
        meansq = jnp.mean(vectors * vectors, axis=-1, keepdims=True)
        vectors = vectors * lax.rsqrt(meansq + EPS) * gain
        vectors = vectors * cosine + pltpu.roll(vectors, HD // 2, 1) * sine
        query = vectors.astype(jnp.bfloat16)
        low, mid, high = [
            lax.dot_general(
                query, k_ref[at, :], (((1,), (1,)), ((), ())), preferred_element_type=jnp.float32
            )
            for at in slices
        ]
        masked = [
            jnp.where(low_keep, low, jnp.float32(-1e30)),
            mid + middle_bias,
            jnp.where(high_keep, high, jnp.float32(-1e30)),
        ]
        tops = [jnp.max(part, axis=-1, keepdims=True) for part in masked]
        top = jnp.maximum(jnp.maximum(tops[0], tops[1]), tops[2])
        expo = [
            jnp.exp2((part - top) * jnp.float32(SCALE * math.log2(math.e))) for part in masked
        ]
        sums = [jnp.sum(part, axis=-1, keepdims=True) for part in expo]
        inverse = 1.0 / (sums[0] + sums[1] + sums[2])
        result = None
        for part, at in zip(expo, slices):
            term = jnp.dot(
                (part * inverse).astype(jnp.bfloat16),
                v_ref[at, :],
                preferred_element_type=jnp.float32,
            )
            result = term if result is None else result + term
        o_ref[:, columns] = result.astype(o_ref.dtype)


def attend(query, gain, cosine, sine, paired, base, row0, count):
    kv_local = query.shape[1] // (GROUP * HD)
    q_tile = 256
    from_tile = row0 // q_tile
    whole = paired.shape[0]
    return pl.pallas_call(
        functools.partial(attend_kernel, q_tile, row0),
        out_shape=jax.ShapeDtypeStruct((count, query.shape[1]), jnp.bfloat16),
        grid=(kv_local, count // q_tile),
        in_specs=[
            pl.BlockSpec(memory_space=pltpu.SMEM),
            pl.BlockSpec((q_tile, GROUP * HD), lambda h, i: (from_tile + i, h)),
            pl.BlockSpec((1, HD), lambda h, i: (0, 0)),
            pl.BlockSpec((q_tile, HD), lambda h, i: (from_tile + i, 0)),
            pl.BlockSpec((q_tile, HD), lambda h, i: (from_tile + i, 0)),
            pl.BlockSpec((whole, HD), lambda h, i: (0, 2 * h)),
            pl.BlockSpec((whole, HD), lambda h, i: (0, 2 * h + 1)),
        ],
        out_specs=pl.BlockSpec((q_tile, GROUP * HD), lambda h, i: (i, h)),
        compiler_params=pltpu.CompilerParams(vmem_limit_bytes=32 * 1024 * 1024),
        cost_estimate=pl.CostEstimate(
            flops=4 * count * query.shape[1] * (WINDOW + q_tile),
            bytes_accessed=4 * (whole + count) * query.shape[1],
            transcendentals=count * query.shape[1] // HD * (WINDOW + q_tile),
        ),
    )(base.reshape(1), query, gain.reshape(1, HD), cosine, sine, paired, paired)


def line_hops(pieces, axis):
    count = lax.axis_size(axis)
    hops = []
    ups = downs = [piece for piece, _ in pieces]
    for step in range(1, count):
        upward = [(i, i + 1) for i in range(step - 1, count - 1)]
        downward = [(i + 1, i) for i in range(count - step)]
        ups = [lax.ppermute(up, axis, upward) for up in ups]
        downs = [lax.ppermute(down, axis, downward) for down in downs]
        hops.append(list(zip(ups, downs)))
    return hops


def line_gather_dot(pieces, hops, weight, axis, depth, column_ranges):
    count = lax.axis_size(axis)
    here = lax.axis_index(axis)

    def terms(totals, piece, owner, first):
        out = []
        for total, (start, width) in zip(totals, column_ranges):
            rows = lax.dynamic_slice(
                weight, (owner * depth + first, start), (piece.shape[1], width)
            )
            term = jnp.dot(piece, rows, preferred_element_type=jnp.float32)
            out.append(term if total is None else total + term)
        return out

    totals = [None] * len(column_ranges)
    for piece, first in pieces:
        totals = terms(totals, piece, here, first)
    for step in range(1, count):
        below = jnp.maximum(here - step, 0)
        above = jnp.minimum(here + step, count - 1)
        for (up, down), (_, first) in zip(hops[step - 1], pieces):
            if step == count - 1 and len(totals) > 1:
                totals, up, down = lax.optimization_barrier((totals, up, down))
            if 2 * step < count:
                totals = terms(totals, up, below, first)
                totals = terms(totals, down, above, first)
            else:
                from_below = here >= step
                totals = terms(
                    totals,
                    jnp.where(from_below, up, down),
                    jnp.where(from_below, below, above),
                    first,
                )
    return totals


def on_device(states, w_qkv, w_out, q_gain, k_gain):
    rows, depth = states.shape
    kv_local = w_qkv.shape[1]
    q_columns = kv_local * GROUP * HD
    kv_columns = kv_local * 2 * HD
    part = depth // PIECES
    pieces = [(states[:, i * part : (i + 1) * part], i * part) for i in range(PIECES)]
    hops = line_hops(pieces, "hid")
    out_whole = lax.all_gather(w_out, "tok", axis=0, tiled=True)
    arranged = jnp.concatenate(
        [
            w_qkv[:, :, : GROUP * HD].reshape(-1, q_columns),
            w_qkv[:, :, GROUP * HD :].reshape(-1, kv_columns),
        ],
        axis=1,
    )
    weight_whole = lax.all_gather(arranged, "tok", axis=0, tiled=True)
    kv, query = line_gather_dot(
        pieces,
        hops,
        weight_whole,
        "hid",
        depth,
        [(q_columns, kv_columns), (0, q_columns)],
    )
    base = lax.axis_index("tok") * rows
    cosine, sine = rope_tables(rows, base)
    paired = norm_rope(kv, k_gain, cosine, sine, 1, 2)
    behind = from_behind(paired[rows - WINDOW :], "tok", 1)
    combined = jnp.concatenate([behind, paired], axis=0)
    results = []
    quarter = rows // 4
    for row0, count in ((0, quarter), (quarter, quarter), (2 * quarter, rows - 2 * quarter)):
        heads = attend(query, q_gain, cosine, sine, combined, base, row0, count)
        (summed,) = line_gather_dot(
            [(heads, 0)],
            line_hops([(heads, 0)], "hid"),
            out_whole,
            "hid",
            heads.shape[1],
            [(0, w_out.shape[1])],
        )
        results.append(summed.astype(jnp.bfloat16))
    return jnp.concatenate(results, axis=0)


def solution(mesh):
    return jax.shard_map(
        on_device,
        mesh=mesh,
        in_specs=(P(("groups", "tok"), "hid"), P("tok", "hid", None), P("tok", "hid"), P(), P()),
        out_specs=P(("groups", "tok"), "hid"),
        check_vma=False,
    )
```

```python
import functools
import math

import jax
import jax.numpy as jnp
from jax import lax
from jax.experimental import pallas as pl
from jax.experimental.pallas import tpu as pltpu
from jax.sharding import PartitionSpec as P

HD = 128
GROUP = 2
WINDOW = 1024


EPS = 1e-06
SCALE = 168.0 ** (-0.5)
ROPE_BASE = 10000.0
PIECES = 2


def from_behind(value, axis, steps):
    count = lax.axis_size(axis)
    first, last = (max(0, -steps), min(count, count - steps))
    return lax.ppermute(value, axis, [(source, source + steps) for source in range(first, last)])


def rope_tables(rows, base):
    half = HD // 2
    inverse = jnp.exp(
        jnp.arange(half, dtype=jnp.float32) * (-2.0 * math.log(ROPE_BASE) / HD)
    )
    pos = base + jnp.arange(rows, dtype=jnp.int32)
    angle = pos.astype(jnp.float32)[:, None] * inverse[None, :]
    cosine, sine = jnp.cos(angle), jnp.sin(angle)
    return (
        jnp.concatenate([cosine, cosine], axis=1),
        jnp.concatenate([-sine, sine], axis=1),
    )


def norm_rope_kernel(rotated, total, x_ref, gain_ref, cos_ref, sin_ref, o_ref):
    gain = gain_ref[...]
    cosine, sine = cos_ref[...], sin_ref[...]
    for head in range(x_ref.shape[1] // HD):
        columns = slice(head * HD, (head + 1) * HD)
        values = x_ref[:, columns]
        if head % total < rotated:
            meansq = jnp.mean(values * values, axis=-1, keepdims=True)
            values = values * lax.rsqrt(meansq + EPS) * gain
            values = values * cosine + pltpu.roll(values, HD // 2, 1) * sine
        o_ref[:, columns] = values.astype(o_ref.dtype)


def norm_rope(values, gain, cosine, sine, rotated, total):
    rows, columns = values.shape
    tile = 256
    row = lambda i: (i, 0)
    return pl.pallas_call(
        functools.partial(norm_rope_kernel, rotated, total),
        out_shape=jax.ShapeDtypeStruct((rows, columns), jnp.bfloat16),
        grid=(rows // tile,),
        in_specs=[
            pl.BlockSpec((tile, columns), row),
            pl.BlockSpec((1, HD), lambda i: (0, 0)),
            pl.BlockSpec((tile, HD), row),
            pl.BlockSpec((tile, HD), row),
        ],
        out_specs=pl.BlockSpec((tile, columns), row),
        cost_estimate=pl.CostEstimate(
            flops=20 * rows * columns, bytes_accessed=6 * rows * columns, transcendentals=0
        ),
    )(values, gain.reshape(1, HD), cosine, sine)


def attend_kernel(q_tile, row0, base_ref, q_ref, gain_ref, cos_ref, sin_ref, k_ref, v_ref, o_ref):
    first = row0 + pl.program_id(1) * q_tile
    parts = ((0, q_tile), (q_tile, WINDOW - q_tile), (WINDOW, q_tile))
    slices = [pl.ds(pl.multiple_of(first + start, q_tile), width) for start, width in parts]
    row = lax.broadcasted_iota(jnp.int32, (q_tile, q_tile), 0)
    column = lax.broadcasted_iota(jnp.int32, (q_tile, q_tile), 1)
    before = WINDOW - 1 - (base_ref[0] + first)
    low_keep = column > jnp.maximum(row, before)
    high_keep = column <= row
    middle = lax.broadcasted_iota(jnp.int32, (1, parts[1][1]), 1) + q_tile
    middle_bias = jnp.where(middle > before, jnp.float32(0.0), jnp.float32(-1e30))
    gain, cosine, sine = gain_ref[...], cos_ref[...], sin_ref[...]
    for member in range(GROUP):
        columns = slice(member * HD, (member + 1) * HD)
        vectors = q_ref[:, columns]
        meansq = jnp.mean(vectors * vectors, axis=-1, keepdims=True)
        vectors = vectors * lax.rsqrt(meansq + EPS) * gain
        vectors = vectors * cosine + pltpu.roll(vectors, HD // 2, 1) * sine
        query = vectors.astype(jnp.bfloat16)
        low, mid, high = [
            lax.dot_general(
                query, k_ref[at, :], (((1,), (1,)), ((), ())), preferred_element_type=jnp.float32
            )
            for at in slices
        ]
        masked = [
            jnp.where(low_keep, low, jnp.float32(-1e30)),
            mid + middle_bias,
            jnp.where(high_keep, high, jnp.float32(-1e30)),
        ]
        tops = [jnp.max(part, axis=-1, keepdims=True) for part in masked]
        top = jnp.maximum(jnp.maximum(tops[0], tops[1]), tops[2])
        expo = [
            jnp.exp2((part - top) * jnp.float32(SCALE * math.log2(math.e))) for part in masked
        ]
        sums = [jnp.sum(part, axis=-1, keepdims=True) for part in expo]
        inverse = 1.0 / (sums[0] + sums[1] + sums[2])
        result = None
        for part, at in zip(expo, slices):
            term = jnp.dot(
                (part * inverse).astype(jnp.bfloat16),
                v_ref[at, :],
                preferred_element_type=jnp.float32,
            )
            result = term if result is None else result + term
        o_ref[:, columns] = result.astype(o_ref.dtype)


def attend(query, gain, cosine, sine, paired, base, row0, count):
    kv_local = query.shape[1] // (GROUP * HD)
    q_tile = 256
    from_tile = row0 // q_tile
    whole = paired.shape[0]
    return pl.pallas_call(
        functools.partial(attend_kernel, q_tile, row0),
        out_shape=jax.ShapeDtypeStruct((count, query.shape[1]), jnp.bfloat16),
        grid=(kv_local, count // q_tile),
        in_specs=[
            pl.BlockSpec(memory_space=pltpu.SMEM),
            pl.BlockSpec((q_tile, GROUP * HD), lambda h, i: (from_tile + i, h)),
            pl.BlockSpec((1, HD), lambda h, i: (0, 0)),
            pl.BlockSpec((q_tile, HD), lambda h, i: (from_tile + i, 0)),
            pl.BlockSpec((q_tile, HD), lambda h, i: (from_tile + i, 0)),
            pl.BlockSpec((whole, HD), lambda h, i: (0, 2 * h)),
            pl.BlockSpec((whole, HD), lambda h, i: (0, 2 * h + 1)),
        ],
        out_specs=pl.BlockSpec((q_tile, GROUP * HD), lambda h, i: (i, h)),
        compiler_params=pltpu.CompilerParams(vmem_limit_bytes=32 * 1024 * 1024),
        cost_estimate=pl.CostEstimate(
            flops=4 * count * query.shape[1] * (WINDOW + q_tile),
            bytes_accessed=4 * (whole + count) * query.shape[1],
            transcendentals=count * query.shape[1] // HD * (WINDOW + q_tile),
        ),
    )(base.reshape(1), query, gain.reshape(1, HD), cosine, sine, paired, paired)


def line_hops(pieces, axis):
    count = lax.axis_size(axis)
    hops = []
    ups = downs = [piece for piece, _ in pieces]
    for step in range(1, count):
        upward = [(i, i + 1) for i in range(step - 1, count - 1)]
        downward = [(i + 1, i) for i in range(count - step)]
        ups = [lax.ppermute(up, axis, upward) for up in ups]
        downs = [lax.ppermute(down, axis, downward) for down in downs]
        hops.append(list(zip(ups, downs)))
    return hops


def line_gather_dot(pieces, hops, weight, axis, depth, column_ranges):
    count = lax.axis_size(axis)
    here = lax.axis_index(axis)

    def terms(totals, piece, owner, first):
        out = []
        for total, (start, width) in zip(totals, column_ranges):
            rows = lax.dynamic_slice(
                weight, (owner * depth + first, start), (piece.shape[1], width)
            )
            term = jnp.dot(piece, rows, preferred_element_type=jnp.float32)
            out.append(term if total is None else total + term)
        return out

    totals = [None] * len(column_ranges)
    for piece, first in pieces:
        totals = terms(totals, piece, here, first)
    for step in range(1, count):
        below = jnp.maximum(here - step, 0)
        above = jnp.minimum(here + step, count - 1)
        for (up, down), (_, first) in zip(hops[step - 1], pieces):
            if step == count - 1 and len(totals) > 1:
                totals, up, down = lax.optimization_barrier((totals, up, down))
            if 2 * step < count:
                totals = terms(totals, up, below, first)
                totals = terms(totals, down, above, first)
            else:
                from_below = here >= step
                totals = terms(
                    totals,
                    jnp.where(from_below, up, down),
                    jnp.where(from_below, below, above),
                    first,
                )
    return totals


def on_device(states, w_qkv, w_out, q_gain, k_gain):
    rows, depth = states.shape
    kv_local = w_qkv.shape[1]
    q_columns = kv_local * GROUP * HD
    kv_columns = kv_local * 2 * HD
    part = depth // PIECES
    pieces = [(states[:, i * part : (i + 1) * part], i * part) for i in range(PIECES)]
    hops = line_hops(pieces, "hid")
    out_whole = lax.all_gather(w_out, "tok", axis=0, tiled=True)
    arranged = jnp.concatenate(
        [
            w_qkv[:, :, : GROUP * HD].reshape(-1, q_columns),
            w_qkv[:, :, GROUP * HD :].reshape(-1, kv_columns),
        ],
        axis=1,
    )
    weight_whole = lax.all_gather(arranged, "tok", axis=0, tiled=True)
    kv, query = line_gather_dot(
        pieces,
        hops,
        weight_whole,
        "hid",
        depth,
        [(q_columns, kv_columns), (0, q_columns)],
    )
    base = lax.axis_index("tok") * rows
    cosine, sine = rope_tables(rows, base)
    paired = norm_rope(kv, k_gain, cosine, sine, 1, 2)
    behind = from_behind(paired[rows - WINDOW :], "tok", 1)
    combined = jnp.concatenate([behind, paired], axis=0)
    results = []
    block = rows // 2
    for row0 in range(0, rows, block):
        heads = attend(query, q_gain, cosine, sine, combined, base, row0, block)
        (summed,) = line_gather_dot(
            [(heads, 0)],
            line_hops([(heads, 0)], "hid"),
            out_whole,
            "hid",
            heads.shape[1],
            [(0, w_out.shape[1])],
        )
        results.append(summed.astype(jnp.bfloat16))
    return jnp.concatenate(results, axis=0)


def solution(mesh):
    return jax.shard_map(
        on_device,
        mesh=mesh,
        in_specs=(P(("groups", "tok"), "hid"), P("tok", "hid", None), P("tok", "hid"), P(), P()),
        out_specs=P(("groups", "tok"), "hid"),
        check_vma=False,
    )
```

```python
import functools
import math

import jax
import jax.numpy as jnp
from jax import lax
from jax.experimental import pallas as pl
from jax.experimental.pallas import tpu as pltpu
from jax.sharding import PartitionSpec as P

HD = 128
GROUP = 2
WINDOW = 1024


EPS = 1e-06
SCALE = 168.0 ** (-0.5)
ROPE_BASE = 10000.0
PIECES = 3


def from_behind(value, axis, steps):
    count = lax.axis_size(axis)
    first, last = (max(0, -steps), min(count, count - steps))
    return lax.ppermute(value, axis, [(source, source + steps) for source in range(first, last)])


def rope_tables(rows, base):
    half = HD // 2
    inverse = jnp.exp(
        jnp.arange(half, dtype=jnp.float32) * (-2.0 * math.log(ROPE_BASE) / HD)
    )
    pos = base + jnp.arange(rows, dtype=jnp.int32)
    angle = pos.astype(jnp.float32)[:, None] * inverse[None, :]
    cosine, sine = jnp.cos(angle), jnp.sin(angle)
    return (
        jnp.concatenate([cosine, cosine], axis=1),
        jnp.concatenate([-sine, sine], axis=1),
    )


def norm_rope_kernel(rotated, total, x_ref, gain_ref, cos_ref, sin_ref, o_ref):
    gain = gain_ref[...]
    cosine, sine = cos_ref[...], sin_ref[...]
    for head in range(x_ref.shape[1] // HD):
        columns = slice(head * HD, (head + 1) * HD)
        values = x_ref[:, columns]
        if head % total < rotated:
            meansq = jnp.mean(values * values, axis=-1, keepdims=True)
            values = values * lax.rsqrt(meansq + EPS) * gain
            values = values * cosine + pltpu.roll(values, HD // 2, 1) * sine
        o_ref[:, columns] = values.astype(o_ref.dtype)


def norm_rope(values, gain, cosine, sine, rotated, total):
    rows, columns = values.shape
    tile = 512
    row = lambda i: (i, 0)
    return pl.pallas_call(
        functools.partial(norm_rope_kernel, rotated, total),
        out_shape=jax.ShapeDtypeStruct((rows, columns), jnp.bfloat16),
        grid=(rows // tile,),
        in_specs=[
            pl.BlockSpec((tile, columns), row),
            pl.BlockSpec((1, HD), lambda i: (0, 0)),
            pl.BlockSpec((tile, HD), row),
            pl.BlockSpec((tile, HD), row),
        ],
        out_specs=pl.BlockSpec((tile, columns), row),
        cost_estimate=pl.CostEstimate(
            flops=20 * rows * columns, bytes_accessed=6 * rows * columns, transcendentals=0
        ),
    )(values, gain.reshape(1, HD), cosine, sine)


def attend_kernel(q_tile, row0, base_ref, q_ref, gain_ref, cos_ref, sin_ref, k_ref, v_ref, o_ref):
    first = row0 + pl.program_id(1) * q_tile
    parts = ((0, q_tile), (q_tile, WINDOW - q_tile), (WINDOW, q_tile))
    slices = [pl.ds(pl.multiple_of(first + start, q_tile), width) for start, width in parts]
    row = lax.broadcasted_iota(jnp.int32, (q_tile, q_tile), 0)
    column = lax.broadcasted_iota(jnp.int32, (q_tile, q_tile), 1)
    before = WINDOW - 1 - (base_ref[0] + first)
    low_keep = column > jnp.maximum(row, before)
    high_keep = column <= row
    middle = lax.broadcasted_iota(jnp.int32, (1, parts[1][1]), 1) + q_tile
    middle_bias = jnp.where(middle > before, jnp.float32(0.0), jnp.float32(-1e30))
    gain, cosine, sine = gain_ref[...], cos_ref[...], sin_ref[...]
    for member in range(GROUP):
        columns = slice(member * HD, (member + 1) * HD)
        vectors = q_ref[:, columns]
        meansq = jnp.mean(vectors * vectors, axis=-1, keepdims=True)
        vectors = vectors * lax.rsqrt(meansq + EPS) * gain
        vectors = vectors * cosine + pltpu.roll(vectors, HD // 2, 1) * sine
        query = vectors.astype(jnp.bfloat16)
        low, mid, high = [
            lax.dot_general(
                query, k_ref[at, :], (((1,), (1,)), ((), ())), preferred_element_type=jnp.float32
            )
            for at in slices
        ]
        masked = [
            jnp.where(low_keep, low, jnp.float32(-1e30)),
            mid + middle_bias,
            jnp.where(high_keep, high, jnp.float32(-1e30)),
        ]
        tops = [jnp.max(part, axis=-1, keepdims=True) for part in masked]
        top = jnp.maximum(jnp.maximum(tops[0], tops[1]), tops[2])
        expo = [
            jnp.exp2((part - top) * jnp.float32(SCALE * math.log2(math.e))) for part in masked
        ]
        sums = [jnp.sum(part, axis=-1, keepdims=True) for part in expo]
        inverse = 1.0 / (sums[0] + sums[1] + sums[2])
        result = None
        for part, at in zip(expo, slices):
            term = jnp.dot(
                (part * inverse).astype(jnp.bfloat16),
                v_ref[at, :],
                preferred_element_type=jnp.float32,
            )
            result = term if result is None else result + term
        o_ref[:, columns] = result.astype(o_ref.dtype)


def attend(query, gain, cosine, sine, paired, base, row0, count):
    kv_local = query.shape[1] // (GROUP * HD)
    q_tile = 256
    from_tile = row0 // q_tile
    whole = paired.shape[0]
    return pl.pallas_call(
        functools.partial(attend_kernel, q_tile, row0),
        out_shape=jax.ShapeDtypeStruct((count, query.shape[1]), jnp.bfloat16),
        grid=(kv_local, count // q_tile),
        in_specs=[
            pl.BlockSpec(memory_space=pltpu.SMEM),
            pl.BlockSpec((q_tile, GROUP * HD), lambda h, i: (from_tile + i, h)),
            pl.BlockSpec((1, HD), lambda h, i: (0, 0)),
            pl.BlockSpec((q_tile, HD), lambda h, i: (from_tile + i, 0)),
            pl.BlockSpec((q_tile, HD), lambda h, i: (from_tile + i, 0)),
            pl.BlockSpec((whole, HD), lambda h, i: (0, 2 * h)),
            pl.BlockSpec((whole, HD), lambda h, i: (0, 2 * h + 1)),
        ],
        out_specs=pl.BlockSpec((q_tile, GROUP * HD), lambda h, i: (i, h)),
        compiler_params=pltpu.CompilerParams(vmem_limit_bytes=32 * 1024 * 1024),
        cost_estimate=pl.CostEstimate(
            flops=4 * count * query.shape[1] * (WINDOW + q_tile),
            bytes_accessed=4 * (whole + count) * query.shape[1],
            transcendentals=count * query.shape[1] // HD * (WINDOW + q_tile),
        ),
    )(base.reshape(1), query, gain.reshape(1, HD), cosine, sine, paired, paired)


def line_hops(pieces, axis):
    count = lax.axis_size(axis)
    hops = []
    ups = downs = [piece for piece, _ in pieces]
    for step in range(1, count):
        upward = [(i, i + 1) for i in range(step - 1, count - 1)]
        downward = [(i + 1, i) for i in range(count - step)]
        ups = [lax.ppermute(up, axis, upward) for up in ups]
        downs = [lax.ppermute(down, axis, downward) for down in downs]
        hops.append(list(zip(ups, downs)))
    return hops


def line_gather_dot(pieces, hops, weight, axis, depth, column_ranges):
    count = lax.axis_size(axis)
    here = lax.axis_index(axis)

    def terms(totals, piece, owner, first):
        out = []
        for total, (start, width) in zip(totals, column_ranges):
            rows = lax.dynamic_slice(
                weight, (owner * depth + first, start), (piece.shape[1], width)
            )
            term = jnp.dot(piece, rows, preferred_element_type=jnp.float32)
            out.append(term if total is None else total + term)
        return out

    totals = [None] * len(column_ranges)
    for piece, first in pieces:
        totals = terms(totals, piece, here, first)
    for step in range(1, count):
        below = jnp.maximum(here - step, 0)
        above = jnp.minimum(here + step, count - 1)
        for (up, down), (_, first) in zip(hops[step - 1], pieces):
            if step == count - 1 and len(totals) > 1:
                totals, up, down = lax.optimization_barrier((totals, up, down))
            if 2 * step < count:
                totals = terms(totals, up, below, first)
                totals = terms(totals, down, above, first)
            else:
                from_below = here >= step
                totals = terms(
                    totals,
                    jnp.where(from_below, up, down),
                    jnp.where(from_below, below, above),
                    first,
                )
    return totals


def on_device(states, w_qkv, w_out, q_gain, k_gain):
    rows, depth = states.shape
    kv_local = w_qkv.shape[1]
    q_columns = kv_local * GROUP * HD
    kv_columns = kv_local * 2 * HD
    part = depth // PIECES
    pieces = [(states[:, i * part : (i + 1) * part], i * part) for i in range(PIECES)]
    hops = line_hops(pieces, "hid")
    out_whole = lax.all_gather(w_out, "tok", axis=0, tiled=True)
    arranged = jnp.concatenate(
        [
            w_qkv[:, :, : GROUP * HD].reshape(-1, q_columns),
            w_qkv[:, :, GROUP * HD :].reshape(-1, kv_columns),
        ],
        axis=1,
    )
    weight_whole = lax.all_gather(arranged, "tok", axis=0, tiled=True)
    kv, query = line_gather_dot(
        pieces,
        hops,
        weight_whole,
        "hid",
        depth,
        [(q_columns, kv_columns), (0, q_columns)],
    )
    base = lax.axis_index("tok") * rows
    cosine, sine = rope_tables(rows, base)
    paired = norm_rope(kv, k_gain, cosine, sine, 1, 2)
    behind = from_behind(paired[rows - WINDOW :], "tok", 1)
    combined = jnp.concatenate([behind, paired], axis=0)
    results = []
    block = rows // 2
    for row0 in range(0, rows, block):
        heads = attend(query, q_gain, cosine, sine, combined, base, row0, block)
        (summed,) = line_gather_dot(
            [(heads, 0)],
            line_hops([(heads, 0)], "hid"),
            out_whole,
            "hid",
            heads.shape[1],
            [(0, w_out.shape[1])],
        )
        results.append(summed.astype(jnp.bfloat16))
    return jnp.concatenate(results, axis=0)


def solution(mesh):
    return jax.shard_map(
        on_device,
        mesh=mesh,
        in_specs=(P(("groups", "tok"), "hid"), P("tok", "hid", None), P("tok", "hid"), P(), P()),
        out_specs=P(("groups", "tok"), "hid"),
        check_vma=False,
    )
```
